32 devices in a mesh: grp: 2 (over y), ep: 4 (over z), tp: 2 (over x), pp: 2 (over core).
Axes of the slice: x: 2, y: 2, z: 4, core: 2. Of those that a mesh axis runs over, the one named last changes fastest.
Arguments:
- queries: bfloat16 [2048, 8192], P(('grp', 'ep', 'pp'), 'tp'), parts along dimension 0, may hold values from -64 to 64
- suffix_keys: bfloat16 [2048, 512], P(('grp', 'ep', 'pp')), parts along dimension 0, may hold values from -6 to 6
- suffix_values: bfloat16 [2048, 512], P(('grp', 'ep', 'pp')), parts along dimension 0, may hold values from -6 to 6
- prefix_keys: bfloat16 [4096, 512], P(('grp', 'ep', 'pp')), parts along dimension 0, may hold values from -8 to 8
- prefix_values: bfloat16 [4096, 512], P(('grp', 'ep', 'pp')), parts along dimension 0, may hold values from -6 to 6
- prefix_groups: int32 [4096], P(('grp', 'ep', 'pp')), parts along dimension 0, may hold values from 0 to 7, never falling along the last dimension, each value on 1 to 1024 neighbouring positions
- shot_counts: int32 [16], P(('grp', 'ep', 'pp')), parts along dimension 0, may hold values from 1 to 8
- lengths: int32 [16], P(('grp', 'ep', 'pp')), parts along dimension 0, may hold values from 32 to 128
- hidden: bfloat16 [2048, 4096], P(('grp', 'ep', 'pp')), parts along dimension 0, may hold values from -6 to 6
- expert_ids: int32 [2048, 8], P(('grp', 'ep')), parts along dimension 0, may hold values from 0 to 127, all different within a row
- gate_weights: float32 [2048, 8], P(('grp', 'ep')), parts along dimension 0, may hold values from 0.1 to 1
- gate_proj: bfloat16 [4, 4096, 1536], P('ep', 'pp', 'tp'), may hold values from -0.09375 to 0.09375
- up_proj: bfloat16 [4, 4096, 1536], P('ep', 'pp', 'tp'), may hold values from -0.09375 to 0.09375
- down_proj: bfloat16 [4, 1536, 4096], P('ep', 'tp', 'pp'), may hold values from -0.15625 to 0.15625
Outputs:
- context: bfloat16 [2048, 8192], P(('grp', 'ep', 'pp'), 'tp'), parts along dimension 0
- moe_out: bfloat16 [2048, 4096], P(('grp', 'ep'), ('pp', 'tp')), parts along dimension 0
The draws below stay inside these ranges and needn't reach their ends.
There are 2 independent parts, one for each index of `grp`. The reference program is written for one: setup_inputs(seed, part) draws one part's arguments, and reference() takes and returns one part's arrays. A program takes and returns all parts, laid end to end along the dimension named above; an argument that names none is the same for every part. Nothing has to cross between parts.
All inputs are finite; a program needn't handle non-finite values.
Results may differ from the reference program's by a relative error of at most 0.022.
Values may be sent and summed in bfloat16 or wider, within the bound.
A program may use at most 128 MiB of HBM per device.

```python
import math
import jax
import jax.numpy as jnp
import numpy as np
from jax import lax

D = 4096
FF = 1536
HEADS = 64
KVH = 4
HD = 128
EXPERTS_ALL = 128
TOP = 8
PREFIX = 2048
SUFFIX = 128
SHOTS = 8
TOK_DEV = 128
SUFFIXES = 8
TOKENS = 1024
EXPERTS = 4
CAP = 12


def draw_queries(key, part):
    values = 1.5 * jax.random.truncated_normal(jax.random.fold_in(key, 11), -6.0, 6.0, (TOKENS, HEADS, HD), jnp.float32)
    return values.reshape(TOKENS, HEADS * HD).astype(jnp.bfloat16)


def draw_prefix_keys(key, part):
    values = jax.random.truncated_normal(jax.random.fold_in(key, 13), -4.0, 4.0, (PREFIX, KVH, HD), jnp.float32)
    return values.reshape(PREFIX, KVH * HD).astype(jnp.bfloat16)


def plant(values, key, least, high):
    place = [jax.random.randint(jax.random.fold_in(key, axis), (), 0, length) for axis, length in enumerate(values.shape)]
    longest = values.shape.index(max(values.shape))
    beside = place[:longest] + [(place[longest] + 1) % values.shape[longest]] + place[longest + 1:]
    return values.at[tuple(place)].set(least).at[tuple(beside)].set(high)


def block_levels(key, extent, split, smallest, top_value):
    factor_of, own = 1.0, jax.random.fold_in(key, 6)
    for dim, blocks in split:
        heights = jnp.exp(jax.random.uniform(jax.random.fold_in(own, dim), (blocks,), jnp.float32, smallest / len(split), top_value / len(split)))
        factor_of = factor_of * jnp.repeat(heights, extent[dim] // blocks).reshape([-1 if axis == dim else 1 for axis in range(len(extent))])
    return factor_of


def different_ones(own_key, rows, amount, top, lift):
    sequence = jax.random.permutation(jax.random.fold_in(own_key, 1), amount)
    pull = sequence
    for power in range(3):
        pull = pull * pull // amount
    pull = pull * lift // amount
    tickets = jax.random.randint(jax.random.fold_in(own_key, 2), (rows, amount), 0, 4096) + pull
    sure = jax.random.permutation(jax.random.fold_in(own_key, 3), rows)[jnp.arange(amount) % rows]
    tickets = jnp.where(jnp.arange(rows)[:, None] == sure[None, :], 1 << 14, tickets)
    score = tickets * amount + jnp.arange(amount)
    return lax.top_k(score.astype(jnp.int32), top)[1].astype(jnp.int32)


def length_profile(amount, total, bound, skew):
    weights = [(1 << 20) // math.isqrt(rank ** skew) + 1 for rank in range(2, amount + 1)]
    surplus, counts = total - bound - (amount - 1), [1] * (amount - 1)
    while surplus > 0:
        movable = [i for i in range(amount - 1) if counts[i] < bound]
        mass, remaining = sum([weights[i] for i in movable]), surplus
        for i in movable:
            addition = min(bound - counts[i], max(1, remaining * weights[i] // mass), surplus)
            counts[i] = counts[i] + addition
            surplus = surplus - addition
    return np.array([bound] + counts)


def uneven_parts(stream_key, amount, total, reach, skew):
    if amount == 2:
        one = jax.random.randint(stream_key, (), max(1, total - reach), min(reach, total - 1) + 1)
        return jnp.stack([one, total - one])
    sizes = jnp.asarray(length_profile(amount, total, reach, skew), jnp.int32)
    twos = (amount - 1) // 2
    source_of, receiver = sizes[1:1 + 2 * twos:2], sizes[2:2 + 2 * twos:2]
    room = jnp.minimum(source_of - 1, reach - receiver)
    moved = jax.random.randint(jax.random.fold_in(stream_key, 1), (twos,), 0, 1 << 20) % (room + 1)
    sizes = sizes.at[1:1 + 2 * twos:2].set(source_of - moved).at[2:2 + 2 * twos:2].set(receiver + moved)
    return sizes[jax.random.permutation(jax.random.fold_in(stream_key, 2), amount)]


def normal_values(key, extent, spread, bound, shards=(), kind=jnp.bfloat16):
    array = jax.random.normal(key, extent, jnp.float32) * spread
    if len(shards) > 0:
        array = block_levels(key, extent, shards, -0.22, 0.18) * array
    return jnp.clip(array, min=-bound, max=bound).astype(kind)


def setup_inputs(seed: int = 0, part: int = 0) -> dict:
    key_list = jax.random.split(jax.random.key(seed), 15)
    part_keys = jax.random.split(jax.random.fold_in(key_list[14], part), 15)
    return {
        "queries": draw_queries(jax.random.fold_in(jax.random.fold_in(key_list[14], part), 71), part),
        "suffix_keys": normal_values(part_keys[1], (TOKENS, KVH * HD), 1.0, 6.0, ((0, 8),)),
        "suffix_values": normal_values(part_keys[2], (TOKENS, KVH * HD), 1.0, 6.0, ((0, 8),)),
        "prefix_keys": draw_prefix_keys(jax.random.fold_in(jax.random.fold_in(key_list[14], part), 71), part),
        "prefix_values": normal_values(part_keys[4], (PREFIX, KVH * HD), 1.0, 6.0, ((0, 8),)),
        "prefix_groups": jnp.searchsorted(jnp.cumsum(uneven_parts(part_keys[5], SHOTS, PREFIX, PREFIX // 2, 1)), jnp.arange(PREFIX), side="right").astype(jnp.int32),
        "shot_counts": plant(jax.random.randint(part_keys[6], (SUFFIXES,), 1, SHOTS + 1), jax.random.fold_in(part_keys[6], 1), 1, SHOTS).astype(jnp.int32),
        "lengths": plant(jax.random.randint(part_keys[7], (SUFFIXES,), SUFFIX // 4, SUFFIX + 1), jax.random.fold_in(part_keys[7], 1), SUFFIX // 4, SUFFIX).astype(jnp.int32),
        "hidden": normal_values(part_keys[8], (TOKENS, D), 1.0, 6.0, ((0, 8),)),
        "expert_ids": different_ones(part_keys[9], TOKENS, EXPERTS_ALL, TOP, 512),
        "gate_weights": jnp.clip(jnp.exp(math.log(1.0) - 2.3025851 * jax.random.uniform(part_keys[10], (TOKENS, TOP), jnp.float32) ** block_levels(part_keys[10], (TOKENS, TOP), ((0, 4),), -0.2, 0.2)), 0.1, 1.0),
        "gate_proj": normal_values(key_list[11], (EXPERTS, D, FF), D ** -0.5, 0.09375, ((0, 4), (1, 2), (2, 2))),
        "up_proj": normal_values(key_list[12], (EXPERTS, D, FF), D ** -0.5, 0.09375, ((0, 4), (1, 2), (2, 2))),
        "down_proj": normal_values(key_list[13], (EXPERTS, FF, D), FF ** -0.5, 0.15625, ((0, 4), (1, 2), (2, 2))),
    }


NEG = -1.0e30


def attend(query_block, suffix_key_block, suffix_value_block, length, shot_count, prefix_keys, prefix_values, prefix_groups):
    head_group = HEADS // KVH
    query_heads = query_block.reshape(SUFFIX, KVH, head_group, HD).astype(jnp.float32)
    key_rows = jnp.concatenate([prefix_keys, suffix_key_block], axis=0).reshape(PREFIX + SUFFIX, KVH, HD).astype(jnp.float32)
    value_rows = jnp.concatenate([prefix_values, suffix_value_block], axis=0).reshape(PREFIX + SUFFIX, KVH, HD).astype(jnp.float32)
    scores = jnp.einsum("tkgd,skd->tkgs", query_heads, key_rows) * (HD ** -0.5)
    position = jnp.arange(SUFFIX, dtype=jnp.int32)
    prefix_seen = jnp.broadcast_to((prefix_groups < shot_count)[None, :], (SUFFIX, PREFIX))
    own_seen = (position[None, :] <= position[:, None]) & (position[None, :] < length)
    visible = jnp.concatenate([prefix_seen, own_seen], axis=1)[:, None, None, :]
    scores = jnp.where(visible, scores, NEG)
    row_max = jnp.max(scores, axis=-1, keepdims=True)
    weights = jnp.where(visible, jnp.exp(scores - row_max), 0.0)
    denominator = jnp.sum(weights, axis=-1)
    rounded = lax.optimization_barrier(weights.astype(jnp.bfloat16)).astype(jnp.float32)
    attended = jnp.einsum("tkgs,skd->tkgd", rounded, value_rows) / denominator[..., None]
    attended = jnp.where((position < length)[:, None, None, None], attended, 0.0)
    return attended.reshape(SUFFIX, HEADS * HD).astype(jnp.bfloat16)


def routing(expert_ids, gate_weights, blocks):
    routed = expert_ids.reshape(blocks, TOK_DEV, TOP)
    gate_share = gate_weights.reshape(blocks, TOK_DEV, TOP)
    matches = routed[..., None] == jnp.arange(EXPERTS, dtype=jnp.int32)
    taken = jnp.sum(matches.astype(jnp.int32), axis=2)
    shares = jnp.sum(jnp.where(matches, gate_share[..., None], 0.0), axis=2)
    slot_index = jnp.cumsum(taken, axis=1) - taken
    served = (taken > 0) & (slot_index < CAP)
    return slot_index, served, shares


def reference(queries, suffix_keys, suffix_values, prefix_keys, prefix_values, prefix_groups, shot_counts, lengths, hidden, expert_ids, gate_weights, gate_proj, up_proj, down_proj):
    def attend_items(items):
        return attend(items[0], items[1], items[2], items[3], items[4], prefix_keys, prefix_values, prefix_groups)

    context = lax.map(attend_items, (queries.reshape(SUFFIXES, SUFFIX, HEADS * HD), suffix_keys.reshape(SUFFIXES, SUFFIX, KVH * HD), suffix_values.reshape(SUFFIXES, SUFFIX, KVH * HD), lengths, shot_counts))
    context = context.reshape(TOKENS, HEADS * HD)

    blocks = TOKENS // TOK_DEV
    slot_index, served, shares = routing(expert_ids, gate_weights, blocks)
    source = jnp.arange(blocks, dtype=jnp.int32)[:, None, None]
    row_index = jnp.where(served, source * CAP + slot_index, blocks * CAP).astype(jnp.int32)
    token_index = jnp.broadcast_to(jnp.arange(TOKENS, dtype=jnp.int32).reshape(blocks, TOK_DEV, 1), row_index.shape)

    def one_expert(expert):
        target = jnp.take(row_index, expert, axis=2).reshape(-1)
        owners = jnp.take(token_index, expert, axis=2).reshape(-1)
        owner = jnp.zeros((blocks * CAP,), jnp.int32).at[target].set(owners, mode="drop")
        filled = jnp.zeros((blocks * CAP,), jnp.bool_).at[target].set(True, mode="drop")
        inputs = jnp.where(filled[:, None], hidden[owner], 0)
        gate = jnp.dot(inputs, gate_proj[expert], preferred_element_type=jnp.float32)
        upward = jnp.dot(inputs, up_proj[expert], preferred_element_type=jnp.float32)
        active = (jax.nn.silu(gate) * upward).astype(jnp.bfloat16)
        return jnp.dot(active, down_proj[expert], preferred_element_type=jnp.float32).astype(jnp.bfloat16)

    expert_out = lax.map(one_expert, jnp.arange(EXPERTS, dtype=jnp.int32))

    def add_expert(running, expert):
        picked = lax.dynamic_index_in_dim(expert_out, expert, 0, keepdims=False)
        gather_rows = jnp.minimum(jnp.take(row_index, expert, axis=2), blocks * CAP - 1).reshape(-1)
        coefficient = jnp.where(jnp.take(served, expert, axis=2), jnp.take(shares, expert, axis=2), 0.0).reshape(-1)
        return running + coefficient[:, None] * picked[gather_rows].astype(jnp.float32), None

    moe_sum, unused_rest = lax.scan(add_expert, jnp.zeros((TOKENS, D), jnp.float32), jnp.arange(EXPERTS, dtype=jnp.int32))
    return context, moe_sum.astype(jnp.bfloat16)
```

```python
import functools
import math

import jax
import jax.numpy as jnp
from jax import lax
from jax.experimental import pallas as pl
from jax.experimental.pallas import tpu as pltpu
from jax.sharding import PartitionSpec as P

D = 4096
HEADS = 64
KVH = 4
HD = 128
TOP = 8
SUFFIX = 128
CAP = 12
PAD = 16
NEG = -1e30
COEF = HD ** (-0.5) * math.log2(math.e)
UNROLL = 4
NT = (((1,), (1,)), ((), ()))
MESH = pl.DeviceIdType.MESH
F32 = jnp.float32
BF16 = jnp.bfloat16


def aligned(value, unit=128):
    return pl.multiple_of(value, unit)


def wide(column_block, width):
    return jnp.concatenate([column_block] * (width // 128), axis=1)


def kernel(
    ep,
    tp,
    q_ref,
    sk_ref,
    sv_ref,
    pk_ref,
    pv_ref,
    pg_ref,
    shots_ref,
    len_ref,
    hid_ref,
    ids_ref,
    gw_ref,
    wg_hbm,
    wu_hbm,
    wd_hbm,
    ctx_ref,
    moe_ref,
    kv,
    kscr,
    vscr,
    ksuf,
    vsuf,
    sbias,
    m_ref,
    acc_ref,
    wg,
    wu,
    wd,
    whi,
    wlo,
    dsend,
    xbuf,
    gown,
    gsend,
    grecv,
    keep,
    tsend,
    trecv,
    rsend,
    rbuf,
    z_up,
    z_dn,
    z_rv,
    p_sd,
    p_rv,
    d_sd,
    d_rv,
    x_sd,
    x_rv,
    g_sd,
    g_rv,
    t_sd,
    t_rv,
    r_sd,
    r_rv,
    w_sem,
):
    z = lax.axis_index("ep")
    x = lax.axis_index("tp")
    c = lax.axis_index("pp")
    me = z * 2 + c
    other = 1 - c
    rows = pk_ref.shape[0]
    heads = q_ref.shape[1] // HD
    group = HEADS // KVH
    kvh = max(1, heads // group)
    per_kv = min(heads, group)
    kvw = kvh * HD
    units = wg.shape[1]
    half = wg.shape[0]
    part = half // tp
    lanes = whi.shape[2]

    barrier = pltpu.get_barrier_semaphore()
    for o in range(1, 2 * ep):
        j = lax.rem(me + o, 2 * ep)
        pl.semaphore_signal(barrier, inc=1, device_id={"ep": j // 2, "pp": j % 2}, device_id_type=MESH)
    for o in range(1, tp):
        pl.semaphore_signal(barrier, inc=1, device_id={"tp": lax.rem(x + o, tp)}, device_id_type=MESH)

    weight_copies = [
        pltpu.make_async_copy(src.at[0], dst, w_sem.at[i])
        for i, (src, dst) in enumerate(((wg_hbm, wg), (wu_hbm, wu), (wd_hbm, wd)))
    ]
    for copy in weight_copies:
        copy.start()

    first = aligned(x * heads // group * HD)
    kv[z, c, 0:rows, :] = pk_ref[:, pl.ds(first, kvw)]
    kv[z, c, rows : 2 * rows, :] = pv_ref[:, pl.ds(first, kvw)]
    ids_row = pg_ref[...].astype(F32)
    if rows < kvw:
        ids_row = jnp.concatenate([ids_row, jnp.zeros((1, kvw - rows), F32)], axis=1)
    kv[z, c, 2 * rows : 2 * rows + 16, :] = jnp.broadcast_to(ids_row, (16, kvw)).astype(BF16)

    lane = lax.broadcasted_iota(jnp.int32, (SUFFIX, lanes), 1)
    expert_of = lax.shift_right_logical(lane, 4)
    slot_of = lane & (PAD - 1)
    usable = (slot_of < CAP) & (lane < ep * PAD)
    below = (
        lax.broadcasted_iota(jnp.int32, (SUFFIX, SUFFIX), 1)
        < lax.broadcasted_iota(jnp.int32, (SUFFIX, SUFFIX), 0)
    )
    below = jnp.where(below, 1.0, 0.0).astype(BF16)
    tables = []
    for b in range(2):
        taken = jnp.zeros((SUFFIX, lanes), F32)
        share = jnp.zeros((SUFFIX, lanes), F32)
        for k in range(TOP):
            named = ids_ref[b * SUFFIX : (b + 1) * SUFFIX, k : k + 1] == expert_of
            taken = jnp.where(named, 1.0, taken)
            share = share + jnp.where(named, gw_ref[b * SUFFIX : (b + 1) * SUFFIX, k : k + 1], 0.0)
        slot = jnp.dot(below, taken.astype(BF16), preferred_element_type=F32)
        hit = (taken > 0.0) & usable & (slot == slot_of.astype(F32))
        tables.append(jnp.where(hit, 1.0, 0.0))
        weight = jnp.where(hit, share, 0.0)
        high = weight.astype(BF16)
        whi[b] = high
        wlo[b] = (weight - high.astype(F32)).astype(BF16)
    own_table = jnp.where(c == 0, tables[0], tables[1])
    pick = own_table.T.astype(BF16)
    for p in range(2):
        columns = aligned(p * half + x * part)
        chosen = jnp.dot(pick, hid_ref[:, pl.ds(columns, part)], preferred_element_type=F32).astype(BF16)
        for e in range(ep):
            dsend[e * 2 + p] = chosen[e * PAD : (e + 1) * PAD]
    xbuf[x, me] = dsend[me]

    pl.semaphore_wait(barrier, 2 * ep - 1 + tp - 1)

    def dispatch_copy(o):
        j = lax.rem(me + o, 2 * ep)
        return pltpu.make_async_remote_copy(
            src_ref=dsend.at[j],
            dst_ref=xbuf.at[x, me],
            send_sem=d_sd.at[o],
            recv_sem=d_rv.at[o],
            device_id={"ep": j // 2, "pp": j % 2},
            device_id_type=MESH,
        )

    def dispatch_arrival(o):
        j = lax.rem(me + 2 * ep - o, 2 * ep)
        return pltpu.make_async_remote_copy(
            src_ref=dsend.at[j],
            dst_ref=xbuf.at[x, j],
            send_sem=d_sd.at[o],
            recv_sem=d_rv.at[o],
            device_id={"ep": j // 2, "pp": j % 2},
            device_id_type=MESH,
        )

    def up_copy(chunk):
        return pltpu.make_async_remote_copy(
            src_ref=kv.at[chunk, c],
            dst_ref=kv.at[chunk, c],
            send_sem=z_up.at[chunk],
            recv_sem=z_rv.at[chunk],
            device_id={"ep": z + 1},
            device_id_type=MESH,
        )

    def down_copy(chunk):
        return pltpu.make_async_remote_copy(
            src_ref=kv.at[chunk, c],
            dst_ref=kv.at[chunk, c],
            send_sem=z_dn.at[chunk],
            recv_sem=z_rv.at[chunk],
            device_id={"ep": z - 1},
            device_id_type=MESH,
        )

    def pair_copy(chunk, core):
        return pltpu.make_async_remote_copy(
            src_ref=kv.at[chunk, core],
            dst_ref=kv.at[chunk, core],
            send_sem=p_sd.at[chunk],
            recv_sem=p_rv.at[chunk],
            device_id={"pp": other},
            device_id_type=MESH,
        )

    pair_copy(z, c).start()
    for o in range(1, 2 * ep):
        dispatch_copy(o).start()

    @pl.when(z < ep - 1)
    def _():
        up_copy(z).start()

    @pl.when(z > 0)
    def _():
        down_copy(z).start()

    def forward_round(s):
        low = z - s
        high = z + s

        @pl.when(low >= 0)
        def _():
            up_copy(low).wait_recv()

            @pl.when(z < ep - 1)
            def _():
                up_copy(low).start()

            pair_copy(low, c).start()

        @pl.when(high <= ep - 1)
        def _():
            down_copy(high).wait_recv()

            @pl.when(z > 0)
            def _():
                down_copy(high).start()

            pair_copy(high, c).start()

    length = len_ref[0]
    shots = shots_ref[0].astype(F32)
    row_id = lax.broadcasted_iota(jnp.int32, (SUFFIX, SUFFIX), 0)
    col_id = lax.broadcasted_iota(jnp.int32, (SUFFIX, SUFFIX), 1)
    sbias[...] = jnp.where((col_id <= row_id) & (col_id < length), 0.0, NEG)
    for g in range(kvh):
        ksuf[g] = sk_ref[:, pl.ds(aligned(first + g * HD), HD)]
        vsuf[g, :, 0:HD] = sv_ref[:, pl.ds(aligned(first + g * HD), HD)]
        vsuf[g, :, HD:] = jnp.ones((SUFFIX, HD), BF16)
        vscr[g, :, HD:] = jnp.ones((2 * rows, HD), BF16)

    unroll = math.gcd(UNROLL, per_kv)

    def own_keys(g):
        @pl.loop(0, per_kv // unroll)
        def _(i):
            for u in range(unroll):
                h = g * per_kv + i * unroll + u
                query = q_ref[:, pl.ds(aligned(h * HD), HD)]
                s = lax.dot_general(query, ksuf[g], NT, preferred_element_type=F32) + sbias[...]
                top = jnp.broadcast_to(jnp.max(s, axis=1, keepdims=True), (SUFFIX, HD))
                weight = jnp.exp2((s - top) * COEF).astype(BF16)
                m_ref[h] = top
                acc_ref[h] = jnp.dot(weight, vsuf[g], preferred_element_type=F32)

    def load_chunk(chunk):
        for core in range(2):
            for g in range(kvh):
                kscr[g, core * rows : (core + 1) * rows, :] = kv[chunk, core, 0:rows, g * HD : (g + 1) * HD]
                vscr[g, core * rows : (core + 1) * rows, 0:HD] = kv[
                    chunk, core, rows : 2 * rows, g * HD : (g + 1) * HD
                ]
        groups = jnp.concatenate(
            [kv[chunk, core, 2 * rows : 2 * rows + 16, :][0:1, 0:rows].astype(F32) for core in range(2)],
            axis=1,
        )
        return jnp.where(groups < shots, 0.0, NEG)

    def prefix_keys(g, bias, last):
        @pl.loop(0, per_kv // unroll)
        def _(i):
            for u in range(unroll):
                h = g * per_kv + i * unroll + u
                columns = pl.ds(aligned(h * HD), HD)
                s = lax.dot_general(q_ref[:, columns], kscr[g], NT, preferred_element_type=F32) + bias
                before = m_ref[h]
                top = jnp.maximum(before, jnp.max(s, axis=1, keepdims=True))
                weight = jnp.exp2((s - wide(top, 2 * rows)) * COEF).astype(BF16)
                factor = jnp.exp2((before - top) * COEF)
                total = acc_ref[h] * wide(factor, 2 * HD) + jnp.dot(
                    weight, vscr[g], preferred_element_type=F32
                )
                if last:
                    mean = total[:, 0:HD] / total[:, HD:]
                    ctx_ref[:, columns] = jnp.where(row_id < length, mean, 0.0).astype(BF16)
                else:
                    m_ref[h] = top
                    acc_ref[h] = total

    def share_copy(o, block):
        return pltpu.make_async_remote_copy(
            src_ref=xbuf.at[block],
            dst_ref=xbuf.at[block],
            send_sem=x_sd.at[o],
            recv_sem=x_rv.at[o],
            device_id={"tp": lax.rem(x + o, tp)},
            device_id_type=MESH,
        )

    def spread():
        for o in range(1, 2 * ep):
            dispatch_arrival(o).wait_recv()
        for o in range(1, tp):
            share_copy(o, x).start()

    sums_copy = pltpu.make_async_remote_copy(
        src_ref=gsend, dst_ref=grecv, send_sem=g_sd.at[0], recv_sem=g_rv.at[0], device_id={"pp": other}, device_id_type=MESH
    )
    tokens = 2 * ep * PAD
    unit_tile = 256 if units % 256 == 0 else units

    def project():
        for o in range(1, tp):
            share_copy(o, lax.rem(x + tp - o, tp)).wait_recv()
        weight_copies[0].wait()
        weight_copies[1].wait()
        for which, w in enumerate((wg, wu)):
            def tile(at, w=w, which=which):
                total = jnp.zeros((tokens, unit_tile), F32)
                for t in range(tp):
                    total = total + jnp.dot(
                        xbuf[t].reshape(tokens, part),
                        w[t * part : (t + 1) * part, at],
                        preferred_element_type=F32,
                    )
                gown[which, :, at] = total
                gsend[which, :, at] = total.astype(BF16)

            if unit_tile == units:
                tile(slice(None))
            else:
                @pl.loop(0, units // unit_tile)
                def _(i, tile=tile):
                    tile(pl.ds(aligned(i * unit_tile), unit_tile))
        sums_copy.start()

    def partial_copy(o):
        return pltpu.make_async_remote_copy(
            src_ref=tsend.at[o],
            dst_ref=trecv.at[o],
            send_sem=t_sd.at[o],
            recv_sem=t_rv.at[o],
            device_id={"tp": lax.rem(x + o, tp)},
            device_id_type=MESH,
        )

    def contract():
        weight_copies[2].wait()
        sums_copy.wait_recv()
        gate = gown[0] + grecv[0].astype(F32)
        up = gown[1] + grecv[1].astype(F32)
        active = (gate / (1.0 + jnp.exp(-gate)) * up).astype(BF16)
        for o in list(range(1, tp)) + [0]:
            base = lax.rem(x + o, tp) * part
            for i in range(part // 256):
                result = jnp.dot(
                    active, wd[:, pl.ds(aligned(base + i * 256), 256)], preferred_element_type=F32
                )
                if o == 0:
                    keep[:, i * 256 : (i + 1) * 256] = result
                else:
                    tsend[o, :, i * 256 : (i + 1) * 256] = result.astype(BF16)
            if o > 0:
                partial_copy(o).start()

    def return_copy(o):
        return pltpu.make_async_remote_copy(
            src_ref=rsend.at[lax.rem(z + o, ep)],
            dst_ref=rbuf.at[z],
            send_sem=r_sd.at[o],
            recv_sem=r_rv.at[o],
            device_id={"ep": lax.rem(z + o, ep)},
            device_id_type=MESH,
        )

    def return_arrival(o):
        source = lax.rem(z + ep - o, ep)
        return pltpu.make_async_remote_copy(
            src_ref=rsend.at[source],
            dst_ref=rbuf.at[source],
            send_sem=r_sd.at[o],
            recv_sem=r_rv.at[o],
            device_id={"ep": source},
            device_id_type=MESH,
        )

    def give_back():
        total = keep[...]
        for o in range(1, tp):
            partial_copy(o).wait_recv()
            total = total + trecv[o].astype(F32)
        rsend[...] = total.astype(BF16).reshape(ep, 2 * PAD, part)
        for o in range(1, ep):
            return_copy(o).start()
        rbuf[z] = rsend[z]

    def combine():
        for o in range(1, ep):
            return_arrival(o).wait_recv()
        for b in range(2):
            served = rbuf[:, b * PAD : (b + 1) * PAD, :].reshape(ep * PAD, part)
            high = whi[b][:, 0 : ep * PAD]
            low = wlo[b][:, 0 : ep * PAD]
            moe_ref[b * SUFFIX : (b + 1) * SUFFIX, :] = (
                jnp.dot(high, served, preferred_element_type=F32)
                + jnp.dot(low, served, preferred_element_type=F32)
            ).astype(BF16)

    phases = [spread, project, contract, give_back, combine]

    for g in range(kvh):
        own_keys(g)

    near = jnp.minimum(z, ep - 1 - z)
    far_sign = jnp.where(z < ep - 1 - z, 1, -1)
    for k in range(ep):
        if k == 0:
            chunk = z
        else:
            forward_round(k)
            both = z + (-1 if k % 2 == 1 else 1) * ((k + 1) // 2)
            chunk = jnp.where(k <= 2 * near, both, z + far_sign * (k - near))
        pair_copy(chunk, other).wait_recv()
        bias = load_chunk(chunk)
        for g in range(kvh):
            prefix_keys(g, bias, k == ep - 1)
            if k == 3 and g == 0 and phases and phases[0] is give_back:
                phases.pop(0)()
        if k < 3 and len(phases) > 2:
            phases.pop(0)()
    while phases:
        phases.pop(0)()

    for o in range(1, 2 * ep):
        dispatch_copy(o).wait_send()
    for o in range(1, tp):
        share_copy(o, x).wait_send()
        partial_copy(o).wait_send()
    for o in range(1, ep):
        return_copy(o).wait_send()
    sums_copy.wait_send()
    for s in range(ep):
        low = z - s
        high = z + s

        @pl.when((low >= 0) & (z < ep - 1))
        def _(low=low):
            up_copy(low).wait_send()

        @pl.when((high <= ep - 1) & (z > 0))
        def _(high=high):
            down_copy(high).wait_send()

        pair_copy(s, c).wait_send()


def shards(ep, tp, queries, suffix_keys, suffix_values, prefix_keys, prefix_values, prefix_groups, shot_counts, lengths, hidden, expert_ids, gate_weights, gate_proj, up_proj, down_proj):
    tok_rows, q_width = queries.shape
    rows = prefix_keys.shape[0]
    heads = q_width // HD
    kvh = max(1, heads // (HEADS // KVH))
    kvw = kvh * HD
    half, units = gate_proj.shape[1:]
    part = half // tp
    lanes = -(-ep * PAD // 128) * 128
    tokens = 2 * ep * PAD
    assert tok_rows == SUFFIX and rows <= kvw
    vmem = pl.BlockSpec(memory_space=pltpu.VMEM)
    smem = pl.BlockSpec(memory_space=pltpu.SMEM)
    hbm = pl.BlockSpec(memory_space=pl.ANY)
    dma = pltpu.SemaphoreType.DMA
    return pl.pallas_call(
        functools.partial(kernel, ep, tp),
        out_shape=(
            jax.ShapeDtypeStruct((tok_rows, q_width), BF16),
            jax.ShapeDtypeStruct((2 * tok_rows, part), BF16),
        ),
        in_specs=[vmem] * 6 + [smem] * 2 + [vmem] * 3 + [hbm] * 3,
        out_specs=(vmem, vmem),
        scratch_shapes=[
            pltpu.VMEM((ep, 2, 2 * rows + 16, kvw), BF16),
            pltpu.VMEM((kvh, 2 * rows, HD), BF16),
            pltpu.VMEM((kvh, 2 * rows, 2 * HD), BF16),
            pltpu.VMEM((kvh, SUFFIX, HD), BF16),
            pltpu.VMEM((kvh, SUFFIX, 2 * HD), BF16),
            pltpu.VMEM((SUFFIX, SUFFIX), F32),
            pltpu.VMEM((heads, SUFFIX, HD), F32),
            pltpu.VMEM((heads, SUFFIX, 2 * HD), F32),
            pltpu.VMEM((half, units), BF16),
            pltpu.VMEM((half, units), BF16),
            pltpu.VMEM((units, half), BF16),
            pltpu.VMEM((2, SUFFIX, lanes), BF16),
            pltpu.VMEM((2, SUFFIX, lanes), BF16),
            pltpu.VMEM((2 * ep, PAD, part), BF16),
            pltpu.VMEM((tp, 2 * ep, PAD, part), BF16),
            pltpu.VMEM((2, tokens, units), F32),
            pltpu.VMEM((2, tokens, units), BF16),
            pltpu.VMEM((2, tokens, units), BF16),
            pltpu.VMEM((tokens, part), F32),
            pltpu.VMEM((tp, tokens, part), BF16),
            pltpu.VMEM((tp, tokens, part), BF16),
            pltpu.VMEM((ep, 2 * PAD, part), BF16),
            pltpu.VMEM((ep, 2 * PAD, part), BF16),
            dma((ep,)),
            dma((ep,)),
            dma((ep,)),
            dma((ep,)),
            dma((ep,)),
            dma((2 * ep,)),
            dma((2 * ep,)),
            dma((tp,)),
            dma((tp,)),
            dma((1,)),
            dma((1,)),
            dma((tp,)),
            dma((tp,)),
            dma((ep,)),
            dma((ep,)),
            dma((3,)),
        ],
        compiler_params=pltpu.CompilerParams(
            collective_id=0, has_side_effects=True, vmem_limit_bytes=50 * 1024 * 1024
        ),
    )(
        queries,
        suffix_keys,
        suffix_values,
        prefix_keys,
        prefix_values,
        prefix_groups.reshape(1, rows),
        shot_counts,
        lengths,
        hidden,
        expert_ids,
        gate_weights,
        gate_proj,
        up_proj,
        down_proj,
    )


def solution(mesh):
    rows = P(("grp", "ep", "pp"), None)
    vector = P(("grp", "ep", "pp"))
    assert mesh.shape["pp"] == 2
    return jax.shard_map(
        functools.partial(shards, mesh.shape["ep"], mesh.shape["tp"]),
        mesh=mesh,
        in_specs=(
            P(("grp", "ep", "pp"), "tp"),
            rows,
            rows,
            rows,
            rows,
            vector,
            vector,
            vector,
            rows,
            P(("grp", "ep"), None),
            P(("grp", "ep"), None),
            P("ep", "pp", "tp"),
            P("ep", "pp", "tp"),
            P("ep", "tp", "pp"),
        ),
        out_specs=(P(("grp", "ep", "pp"), "tp"), P(("grp", "ep"), ("pp", "tp"))),
        check_vma=False,
    )
```

```python
import functools
import math

import jax
import jax.numpy as jnp
from jax import lax
from jax.experimental import pallas as pl
from jax.experimental.pallas import tpu as pltpu
from jax.sharding import PartitionSpec as P

D = 4096
HEADS = 64
KVH = 4
HD = 128
TOP = 8
SUFFIX = 128
CAP = 12
PAD = 16
NEG = -1e30
COEF = HD ** (-0.5) * math.log2(math.e)
STACK = 2
SLOTS = 2
NT = (((1,), (1,)), ((), ()))
MESH = pl.DeviceIdType.MESH
F32 = jnp.float32
BF16 = jnp.bfloat16


def block_of(per_kv):
    stack = math.gcd(STACK, per_kv)
    return stack, math.gcd(SLOTS, per_kv // stack)


def aligned(value, unit=128):
    return pl.multiple_of(value, unit)


def wide(column_block, width):
    return jnp.concatenate([column_block] * (width // 128), axis=1)


def kernel(
    ep,
    tp,
    q_hbm,
    sk_hbm,
    sv_hbm,
    pk_hbm,
    pv_hbm,
    pg_ref,
    shots_ref,
    len_ref,
    hid_hbm,
    ids_ref,
    gw_ref,
    wg_hbm,
    wu_hbm,
    wd_hbm,
    ctx_ref,
    moe_ref,
    kv,
    kscr,
    vscr,
    ksuf,
    vsuf,
    sbias,
    q_ref,
    sk_ref,
    sv_ref,
    pk_ref,
    pv_ref,
    hid_ref,
    qs,
    m_refs,
    acc_refs,
    wg,
    wu,
    wd,
    whi,
    wlo,
    dsend,
    xbuf,
    gown,
    gsend,
    grecv,
    keep,
    tsend,
    trecv,
    rsend,
    rbuf,
    z_up,
    z_dn,
    z_rv,
    p_sd,
    p_rv,
    d_sd,
    d_rv,
    x_sd,
    x_rv,
    g_sd,
    g_rv,
    t_sd,
    t_rv,
    r_sd,
    r_rv,
    w_sem,
    i_sem,
):
    z = lax.axis_index("ep")
    x = lax.axis_index("tp")
    c = lax.axis_index("pp")
    me = z * 2 + c
    other = 1 - c
    rows = pk_hbm.shape[0]
    heads = q_hbm.shape[1] // HD
    group = HEADS // KVH
    kvh = max(1, heads // group)
    per_kv = min(heads, group)
    kvw = kvh * HD
    units = wg.shape[1]
    half = wg.shape[0]
    part = half // tp
    lanes = whi.shape[2]

    barrier = pltpu.get_barrier_semaphore()
    for o in range(1, 2 * ep):
        j = lax.rem(me + o, 2 * ep)
        pl.semaphore_signal(barrier, inc=1, device_id={"ep": j // 2, "pp": j % 2}, device_id_type=MESH)
    for o in range(1, tp):
        pl.semaphore_signal(barrier, inc=1, device_id={"tp": lax.rem(x + o, tp)}, device_id_type=MESH)

    first = aligned(x * heads // group * HD)
    own_columns = pl.ds(first, kvw)
    input_copies = [
        pltpu.make_async_copy(src, dst, i_sem.at[i])
        for i, (src, dst) in enumerate(
            (
                (pk_hbm.at[:, own_columns], pk_ref),
                (pv_hbm.at[:, own_columns], pv_ref),
                (hid_hbm.at[:, pl.ds(aligned(x * part), part)], hid_ref.at[0]),
                (hid_hbm.at[:, pl.ds(aligned(half + x * part), part)], hid_ref.at[1]),
                (sk_hbm.at[:, own_columns], sk_ref),
                (sv_hbm.at[:, own_columns], sv_ref),
                (q_hbm, q_ref),
            )
        )
    ]
    for copy in input_copies:
        copy.start()
    weight_copies = [
        pltpu.make_async_copy(src.at[0], dst, w_sem.at[i])
        for i, (src, dst) in enumerate(((wg_hbm, wg), (wu_hbm, wu), (wd_hbm, wd)))
    ]
    for copy in weight_copies:
        copy.start()

    for copy in input_copies[0:2]:
        copy.wait()
    kv[z, c, 0:rows, :] = pk_ref[...]
    kv[z, c, rows : 2 * rows, :] = pv_ref[...]
    ids_row = pg_ref[...].astype(F32)
    if rows < kvw:
        ids_row = jnp.concatenate([ids_row, jnp.zeros((1, kvw - rows), F32)], axis=1)
    kv[z, c, 2 * rows : 2 * rows + 16, :] = jnp.broadcast_to(ids_row, (16, kvw)).astype(BF16)

    line = lax.broadcasted_iota(jnp.int32, (lanes, SUFFIX), 0)
    expert_of = lax.shift_right_logical(line, 4)
    slot_of = line & (PAD - 1)
    usable = (slot_of < CAP) & (line < ep * PAD)
    earlier = (
        lax.broadcasted_iota(jnp.int32, (SUFFIX, SUFFIX), 0)
        < lax.broadcasted_iota(jnp.int32, (SUFFIX, SUFFIX), 1)
    )
    earlier = jnp.where(earlier, 1.0, 0.0).astype(BF16)
    tables = []
    for b in range(2):
        taken = jnp.zeros((lanes, SUFFIX), F32)
        share = jnp.zeros((lanes, SUFFIX), F32)
        for k in range(TOP):
            named = ids_ref[k : k + 1, b * SUFFIX : (b + 1) * SUFFIX] == expert_of
            taken = jnp.where(named, 1.0, taken)
            share = share + jnp.where(named, gw_ref[k : k + 1, b * SUFFIX : (b + 1) * SUFFIX], 0.0)
        slot = jnp.dot(taken.astype(BF16), earlier, preferred_element_type=F32)
        hit = (taken > 0.0) & usable & (slot == slot_of.astype(F32))
        tables.append(jnp.where(hit, 1.0, 0.0))
        weight = jnp.where(hit, share, 0.0).T
        upper = weight.astype(BF16)
        whi[b] = upper
        wlo[b] = (weight - upper.astype(F32)).astype(BF16)
    pick = jnp.where(c == 0, tables[0], tables[1]).astype(BF16)
    for copy in input_copies[2:4]:
        copy.wait()
    for p in range(2):
        chosen = jnp.dot(pick, hid_ref[p], preferred_element_type=F32).astype(BF16)
        for e in range(ep):
            dsend[e * 2 + p] = chosen[e * PAD : (e + 1) * PAD]
    xbuf[x, me] = dsend[me]

    pl.semaphore_wait(barrier, 2 * ep - 1 + tp - 1)

    def dispatch_copy(o):
        j = lax.rem(me + o, 2 * ep)
        return pltpu.make_async_remote_copy(
            src_ref=dsend.at[j],
            dst_ref=xbuf.at[x, me],
            send_sem=d_sd.at[o],
            recv_sem=d_rv.at[o],
            device_id={"ep": j // 2, "pp": j % 2},
            device_id_type=MESH,
        )

    def dispatch_arrival(o):
        j = lax.rem(me + 2 * ep - o, 2 * ep)
        return pltpu.make_async_remote_copy(
            src_ref=dsend.at[j],
            dst_ref=xbuf.at[x, j],
            send_sem=d_sd.at[o],
            recv_sem=d_rv.at[o],
            device_id={"ep": j // 2, "pp": j % 2},
            device_id_type=MESH,
        )

    def up_copy(chunk):
        return pltpu.make_async_remote_copy(
            src_ref=kv.at[chunk, c],
            dst_ref=kv.at[chunk, c],
            send_sem=z_up.at[chunk],
            recv_sem=z_rv.at[chunk],
            device_id={"ep": z + 1},
            device_id_type=MESH,
        )

    def down_copy(chunk):
        return pltpu.make_async_remote_copy(
            src_ref=kv.at[chunk, c],
            dst_ref=kv.at[chunk, c],
            send_sem=z_dn.at[chunk],
            recv_sem=z_rv.at[chunk],
            device_id={"ep": z - 1},
            device_id_type=MESH,
        )

    def pair_copy(chunk, core):
        return pltpu.make_async_remote_copy(
            src_ref=kv.at[chunk, core],
            dst_ref=kv.at[chunk, core],
            send_sem=p_sd.at[chunk],
            recv_sem=p_rv.at[chunk],
            device_id={"pp": other},
            device_id_type=MESH,
        )

    pair_copy(z, c).start()
    for o in range(1, 2 * ep):
        dispatch_copy(o).start()

    @pl.when(z < ep - 1)
    def _():
        up_copy(z).start()

    @pl.when(z > 0)
    def _():
        down_copy(z).start()

    def forward_round(s):
        low = z - s
        high = z + s

        @pl.when(low >= 0)
        def _():
            up_copy(low).wait_recv()

            @pl.when(z < ep - 1)
            def _():
                up_copy(low).start()

            pair_copy(low, c).start()

        @pl.when(high <= ep - 1)
        def _():
            down_copy(high).wait_recv()

            @pl.when(z > 0)
            def _():
                down_copy(high).start()

            pair_copy(high, c).start()

    for copy in input_copies[4:]:
        copy.wait()
    for h in range(heads):
        qs[h] = q_ref[:, h * HD : (h + 1) * HD]
    length = len_ref[0]
    shots = shots_ref[0].astype(F32)
    row_id = lax.broadcasted_iota(jnp.int32, (SUFFIX, SUFFIX), 0)
    col_id = lax.broadcasted_iota(jnp.int32, (SUFFIX, SUFFIX), 1)
    sbias[...] = jnp.where((col_id <= row_id) & (col_id < length), 0.0, NEG)
    for g in range(kvh):
        ksuf[g] = sk_ref[:, g * HD : (g + 1) * HD]
        vsuf[g, :, 0:HD] = sv_ref[:, g * HD : (g + 1) * HD]
        vsuf[g, :, HD:] = jnp.ones((SUFFIX, HD), BF16)
        vscr[g, :, HD:] = jnp.ones((2 * rows, HD), BF16)

    stack, slots = block_of(per_kv)
    step = stack * slots
    high = stack * SUFFIX

    def own_keys(g):
        @pl.loop(0, per_kv // step)
        def _(i):
            for u in range(slots):
                b = g * (per_kv // step) + i
                query = qs[pl.ds(b * step + u * stack, stack)].reshape(high, HD)
                s = lax.dot_general(query, ksuf[g], NT, preferred_element_type=F32)
                s = (s.reshape(stack, SUFFIX, SUFFIX) + sbias[...]).reshape(high, SUFFIX)
                top = jnp.broadcast_to(jnp.max(s, axis=1, keepdims=True), (high, HD))
                weight = jnp.exp2((s - top) * COEF).astype(BF16)
                m_refs[u][b] = top
                acc_refs[u][b] = jnp.dot(weight, vsuf[g], preferred_element_type=F32)

    def load_chunk(chunk):
        for core in range(2):
            for g in range(kvh):
                kscr[g, core * rows : (core + 1) * rows, :] = kv[chunk, core, 0:rows, g * HD : (g + 1) * HD]
                vscr[g, core * rows : (core + 1) * rows, 0:HD] = kv[
                    chunk, core, rows : 2 * rows, g * HD : (g + 1) * HD
                ]
        groups = jnp.concatenate(
            [kv[chunk, core, 2 * rows : 2 * rows + 16, :][0:1, 0:rows].astype(F32) for core in range(2)],
            axis=1,
        )
        return jnp.where(groups < shots, 0.0, NEG)

    def prefix_keys(g, bias, last):
        @pl.loop(0, per_kv // step)
        def _(i):
            b = g * (per_kv // step) + i
            for u in range(slots):
                query = qs[pl.ds(b * step + u * stack, stack)].reshape(high, HD)
                s = lax.dot_general(query, kscr[g], NT, preferred_element_type=F32) + bias
                before = m_refs[u][b]
                top = jnp.maximum(before, jnp.max(s, axis=1, keepdims=True))
                weight = jnp.exp2((s - wide(top, 2 * rows)) * COEF).astype(BF16)
                factor = jnp.exp2((before - top) * COEF)
                total = acc_refs[u][b] * wide(factor, 2 * HD) + jnp.dot(
                    weight, vscr[g], preferred_element_type=F32
                )
                if last:
                    mean = total[:, 0:HD] / total[:, HD:]
                    for t in range(stack):
                        block = mean[t * SUFFIX : (t + 1) * SUFFIX]
                        columns = pl.ds(aligned((b * step + u * stack + t) * HD), HD)
                        ctx_ref[:, columns] = jnp.where(row_id < length, block, 0.0).astype(BF16)
                else:
                    m_refs[u][b] = top
                    acc_refs[u][b] = total

    def share_copy(o, block):
        return pltpu.make_async_remote_copy(
            src_ref=xbuf.at[block],
            dst_ref=xbuf.at[block],
            send_sem=x_sd.at[o],
            recv_sem=x_rv.at[o],
            device_id={"tp": lax.rem(x + o, tp)},
            device_id_type=MESH,
        )

    def spread():
        for o in range(1, 2 * ep):
            dispatch_arrival(o).wait_recv()
        for o in range(1, tp):
            share_copy(o, x).start()

    sums_copy = pltpu.make_async_remote_copy(
        src_ref=gsend, dst_ref=grecv, send_sem=g_sd.at[0], recv_sem=g_rv.at[0], device_id={"pp": other}, device_id_type=MESH
    )
    tokens = 2 * ep * PAD
    unit_tile = 256 if units % 256 == 0 else units

    def project():
        for o in range(1, tp):
            share_copy(o, lax.rem(x + tp - o, tp)).wait_recv()
        weight_copies[0].wait()
        weight_copies[1].wait()
        for which, w in enumerate((wg, wu)):
            def tile(at, w=w, which=which):
                total = jnp.zeros((tokens, unit_tile), F32)
                for t in range(tp):
                    total = total + jnp.dot(
                        xbuf[t].reshape(tokens, part),
                        w[t * part : (t + 1) * part, at],
                        preferred_element_type=F32,
                    )
                gown[which, :, at] = total
                gsend[which, :, at] = total.astype(BF16)

            if unit_tile == units:
                tile(slice(None))
            else:
                @pl.loop(0, units // unit_tile)
                def _(i, tile=tile):
                    tile(pl.ds(aligned(i * unit_tile), unit_tile))
        sums_copy.start()

    def partial_copy(o):
        return pltpu.make_async_remote_copy(
            src_ref=tsend.at[o],
            dst_ref=trecv.at[o],
            send_sem=t_sd.at[o],
            recv_sem=t_rv.at[o],
            device_id={"tp": lax.rem(x + o, tp)},
            device_id_type=MESH,
        )

    def contract():
        weight_copies[2].wait()
        sums_copy.wait_recv()
        gate = gown[0] + grecv[0].astype(F32)
        up = gown[1] + grecv[1].astype(F32)
        active = (gate / (1.0 + jnp.exp(-gate)) * up).astype(BF16)
        for o in list(range(1, tp)) + [0]:
            base = lax.rem(x + o, tp) * part
            for i in range(part // 256):
                result = jnp.dot(
                    active, wd[:, pl.ds(aligned(base + i * 256), 256)], preferred_element_type=F32
                )
                if o == 0:
                    keep[:, i * 256 : (i + 1) * 256] = result
                else:
                    tsend[o, :, i * 256 : (i + 1) * 256] = result.astype(BF16)
            if o > 0:
                partial_copy(o).start()

    def return_copy(o):
        return pltpu.make_async_remote_copy(
            src_ref=rsend.at[lax.rem(z + o, ep)],
            dst_ref=rbuf.at[z],
            send_sem=r_sd.at[o],
            recv_sem=r_rv.at[o],
            device_id={"ep": lax.rem(z + o, ep)},
            device_id_type=MESH,
        )

    def return_arrival(o):
        source = lax.rem(z + ep - o, ep)
        return pltpu.make_async_remote_copy(
            src_ref=rsend.at[source],
            dst_ref=rbuf.at[source],
            send_sem=r_sd.at[o],
            recv_sem=r_rv.at[o],
            device_id={"ep": source},
            device_id_type=MESH,
        )

    def give_back():
        total = keep[...]
        for o in range(1, tp):
            partial_copy(o).wait_recv()
            total = total + trecv[o].astype(F32)
        rsend[...] = total.astype(BF16).reshape(ep, 2 * PAD, part)
        for o in range(1, ep):
            return_copy(o).start()
        rbuf[z] = rsend[z]

    def combine():
        for o in range(1, ep):
            return_arrival(o).wait_recv()
        for b in range(2):
            served = rbuf[:, b * PAD : (b + 1) * PAD, :].reshape(ep * PAD, part)
            high = whi[b][:, 0 : ep * PAD]
            low = wlo[b][:, 0 : ep * PAD]
            moe_ref[b * SUFFIX : (b + 1) * SUFFIX, :] = (
                jnp.dot(high, served, preferred_element_type=F32)
                + jnp.dot(low, served, preferred_element_type=F32)
            ).astype(BF16)

    phases = [spread, project, contract, give_back, combine]

    for g in range(kvh):
        own_keys(g)

    near = jnp.minimum(z, ep - 1 - z)
    far_sign = jnp.where(z < ep - 1 - z, 1, -1)
    for k in range(ep):
        if k == 0:
            chunk = z
        else:
            forward_round(k)
            both = z + (-1 if k % 2 == 1 else 1) * ((k + 1) // 2)
            chunk = jnp.where(k <= 2 * near, both, z + far_sign * (k - near))
        pair_copy(chunk, other).wait_recv()
        bias = load_chunk(chunk)
        for g in range(kvh):
            prefix_keys(g, bias, k == ep - 1)
            if k == 3 and g == 0 and phases and phases[0] is give_back:
                phases.pop(0)()
        if k < 3 and len(phases) > 2:
            phases.pop(0)()
    while phases:
        phases.pop(0)()

    for o in range(1, 2 * ep):
        dispatch_copy(o).wait_send()
    for o in range(1, tp):
        share_copy(o, x).wait_send()
        partial_copy(o).wait_send()
    for o in range(1, ep):
        return_copy(o).wait_send()
    sums_copy.wait_send()
    for s in range(ep):
        low = z - s
        high = z + s

        @pl.when((low >= 0) & (z < ep - 1))
        def _(low=low):
            up_copy(low).wait_send()

        @pl.when((high <= ep - 1) & (z > 0))
        def _(high=high):
            down_copy(high).wait_send()

        pair_copy(s, c).wait_send()


def shards(ep, tp, queries, suffix_keys, suffix_values, prefix_keys, prefix_values, prefix_groups, shot_counts, lengths, hidden, expert_ids, gate_weights, gate_proj, up_proj, down_proj):
    tok_rows, q_width = queries.shape
    rows = prefix_keys.shape[0]
    heads = q_width // HD
    kvh = max(1, heads // (HEADS // KVH))
    kvw = kvh * HD
    half, units = gate_proj.shape[1:]
    part = half // tp
    lanes = -(-ep * PAD // 128) * 128
    tokens = 2 * ep * PAD
    assert tok_rows == SUFFIX and rows <= kvw
    stack, slots = block_of(min(heads, HEADS // KVH))
    step = stack * slots
    vmem = pl.BlockSpec(memory_space=pltpu.VMEM)
    smem = pl.BlockSpec(memory_space=pltpu.SMEM)
    hbm = pl.BlockSpec(memory_space=pl.ANY)
    dma = pltpu.SemaphoreType.DMA
    return pl.pallas_call(
        functools.partial(kernel, ep, tp),
        out_shape=(
            jax.ShapeDtypeStruct((tok_rows, q_width), BF16),
            jax.ShapeDtypeStruct((2 * tok_rows, part), BF16),
        ),
        in_specs=[hbm] * 5 + [vmem] + [smem] * 2 + [hbm] + [vmem] * 2 + [hbm] * 3,
        out_specs=(vmem, vmem),
        scratch_shapes=[
            pltpu.VMEM((ep, 2, 2 * rows + 16, kvw), BF16),
            pltpu.VMEM((kvh, 2 * rows, HD), BF16),
            pltpu.VMEM((kvh, 2 * rows, 2 * HD), BF16),
            pltpu.VMEM((kvh, SUFFIX, HD), BF16),
            pltpu.VMEM((kvh, SUFFIX, 2 * HD), BF16),
            pltpu.VMEM((SUFFIX, SUFFIX), F32),
            pltpu.VMEM((tok_rows, q_width), BF16),
            pltpu.VMEM((tok_rows, kvw), BF16),
            pltpu.VMEM((tok_rows, kvw), BF16),
            pltpu.VMEM((rows, kvw), BF16),
            pltpu.VMEM((rows, kvw), BF16),
            pltpu.VMEM((2, tok_rows, part), BF16),
            pltpu.VMEM((heads, SUFFIX, HD), BF16),
            [pltpu.VMEM((heads // step, stack * SUFFIX, HD), F32)] * slots,
            [pltpu.VMEM((heads // step, stack * SUFFIX, 2 * HD), F32)] * slots,
            pltpu.VMEM((half, units), BF16),
            pltpu.VMEM((half, units), BF16),
            pltpu.VMEM((units, half), BF16),
            pltpu.VMEM((2, SUFFIX, lanes), BF16),
            pltpu.VMEM((2, SUFFIX, lanes), BF16),
            pltpu.VMEM((2 * ep, PAD, part), BF16),
            pltpu.VMEM((tp, 2 * ep, PAD, part), BF16),
            pltpu.VMEM((2, tokens, units), F32),
            pltpu.VMEM((2, tokens, units), BF16),
            pltpu.VMEM((2, tokens, units), BF16),
            pltpu.VMEM((tokens, part), F32),
            pltpu.VMEM((tp, tokens, part), BF16),
            pltpu.VMEM((tp, tokens, part), BF16),
            pltpu.VMEM((ep, 2 * PAD, part), BF16),
            pltpu.VMEM((ep, 2 * PAD, part), BF16),
            dma((ep,)),
            dma((ep,)),
            dma((ep,)),
            dma((ep,)),
            dma((ep,)),
            dma((2 * ep,)),
            dma((2 * ep,)),
            dma((tp,)),
            dma((tp,)),
            dma((1,)),
            dma((1,)),
            dma((tp,)),
            dma((tp,)),
            dma((ep,)),
            dma((ep,)),
            dma((3,)),
            dma((7,)),
        ],
        compiler_params=pltpu.CompilerParams(
            collective_id=0, has_side_effects=True, vmem_limit_bytes=56 * 1024 * 1024
        ),
    )(
        queries,
        suffix_keys,
        suffix_values,
        prefix_keys,
        prefix_values,
        prefix_groups.reshape(1, rows),
        shot_counts,
        lengths,
        hidden,
        expert_ids.T,
        gate_weights.T,
        gate_proj,
        up_proj,
        down_proj,
    )


def solution(mesh):
    rows = P(("grp", "ep", "pp"), None)
    vector = P(("grp", "ep", "pp"))
    assert mesh.shape["pp"] == 2
    return jax.shard_map(
        functools.partial(shards, mesh.shape["ep"], mesh.shape["tp"]),
        mesh=mesh,
        in_specs=(
            P(("grp", "ep", "pp"), "tp"),
            rows,
            rows,
            rows,
            rows,
            vector,
            vector,
            vector,
            rows,
            P(("grp", "ep"), None),
            P(("grp", "ep"), None),
            P("ep", "pp", "tp"),
            P("ep", "pp", "tp"),
            P("ep", "tp", "pp"),
        ),
        out_specs=(P(("grp", "ep", "pp"), "tp"), P(("grp", "ep"), ("pp", "tp"))),
        check_vma=False,
    )
```
